32 devices in a mesh: groups: 2 (over y), blk: 4 (over z), inner: 4 (over x, core).
Axes of the slice: x: 2, y: 2, z: 4, core: 2. Of those that a mesh axis runs over, the one named last changes fastest.
Arguments:
- tokens: bfloat16 [1536, 2048], P(('groups', 'blk'), 'inner'), parts along dimension 0, may hold values from -6 to 6
- out_grad: bfloat16 [1536, 2048], P(('groups', 'blk'), 'inner'), parts along dimension 0, may hold values from -0.29882812 to 0.29882812
- w_gate: bfloat16 [8192, 2048], P(('blk', 'inner')), may hold values from -0.125 to 0.125
- w_up: bfloat16 [8192, 2048], P(('blk', 'inner')), may hold values from -0.125 to 0.125
- w_down: bfloat16 [8192, 2048], P(('blk', 'inner')), may hold values from -0.0625 to 0.0625
Outputs:
- mixed: bfloat16 [1536, 2048], P(('groups', 'blk'), 'inner'), parts along dimension 0
- grad_gate: float32 [16384, 2048], P(('groups', 'blk', 'inner')), parts along dimension 0
- grad_up: float32 [16384, 2048], P(('groups', 'blk', 'inner')), parts along dimension 0
- grad_down: float32 [16384, 2048], P(('groups', 'blk', 'inner')), parts along dimension 0
The draws below stay inside these ranges and needn't reach their ends.
There are 2 independent parts, one for each index of `groups`. The reference program is written for one: setup_inputs(seed, part) draws one part's arguments, and reference() takes and returns one part's arrays. A program takes and returns all parts, laid end to end along the dimension named above; an argument that names none is the same for every part. Nothing has to cross between parts.
All inputs are finite; a program needn't handle non-finite values.
Results may differ from the reference program's by a relative error of at most 0.0051.
Values may be sent and summed in bfloat16 or wider, within the bound.
A program may use at most 128 MiB of HBM per device.

```python
import jax
import jax.numpy as jnp
from jax import lax

D = 2048
FF = 8192
ROWS = 192
BWD_STEPS = 2
SLAB = 2048
TOKENS = 768
N_BLK = 4


def steps_of(own_key, extent, split, low, top_value):
    level, own = 1.0, jax.random.fold_in(own_key, 6)
    for position, blocks in split:
        draws = jnp.exp(jax.random.uniform(jax.random.fold_in(own, position), (blocks,), jnp.float32, low / len(split), top_value / len(split)))
        level = level * jnp.repeat(draws, extent[position] // blocks).reshape([-1 if axis == position else 1 for axis in range(len(extent))])
    return level


def bell_draw(key, extent, scale, bound, pieces=(), kind=jnp.bfloat16):
    level = steps_of(key, extent, pieces, -0.22, 0.18) if pieces else 1.0
    entries = jax.random.normal(key, extent, jnp.float32) * scale * level
    return jnp.minimum(jnp.maximum(entries, -bound), bound).astype(kind)


def setup_inputs(seed: int = 0, part: int = 0) -> dict:
    arg_keys = jax.random.split(jax.random.key(seed), 6)
    part_splits = jax.random.split(jax.random.fold_in(arg_keys[5], part), 6)
    return {
        "tokens": bell_draw(part_splits[0], (TOKENS, D), 1.0, 6.0, ((0, 4), (1, 4))),
        "out_grad": bell_draw(part_splits[1], (TOKENS, D), 0.05, 0.29882812, ((0, 4), (1, 4))),
        "w_gate": bell_draw(arg_keys[2], (FF, D), D ** -0.5, 0.125, ((0, 16),)),
        "w_up": bell_draw(arg_keys[3], (FF, D), D ** -0.5, 0.125, ((0, 16),)),
        "w_down": bell_draw(arg_keys[4], (FF, D), FF ** -0.5, 0.0625, ((0, 16),)),
    }


def slab_rows(slab, rows):
    return lax.dot_general(slab, rows, (((1,), (1,)), ((), ())), preferred_element_type=jnp.float32)


def grad_term(rows, grads, gate_slab, up_slab, down_slab):
    gate_t = slab_rows(gate_slab, rows)
    up_t = slab_rows(up_slab, rows)
    sigma = jax.nn.sigmoid(gate_t)
    active = gate_t * sigma
    hidden = (active * up_t).astype(jnp.bfloat16)
    back = slab_rows(down_slab, grads)
    dgate = (back * up_t * sigma * (1.0 + gate_t * (1.0 - sigma))).astype(jnp.bfloat16)
    dup = (back * active).astype(jnp.bfloat16)
    gate_part = jnp.dot(dgate, rows, preferred_element_type=jnp.float32)
    up_part = jnp.dot(dup, rows, preferred_element_type=jnp.float32)
    down_part = jnp.dot(hidden, grads, preferred_element_type=jnp.float32)
    return gate_part, up_part, down_part


def reference(tokens, out_grad, w_gate, w_up, w_down):
    blocks = tokens.reshape(N_BLK, ROWS, D)
    grad_blocks = out_grad.reshape(N_BLK, ROWS, D)
    gate_slabs = w_gate.reshape(N_BLK, SLAB, D)
    up_slabs = w_up.reshape(N_BLK, SLAB, D)
    down_slabs = w_down.reshape(N_BLK, SLAB, D)

    def pick(table, index):
        return lax.dynamic_index_in_dim(table, index.astype(jnp.int32), 0, keepdims=False)

    def forward_block(rows):
        gate_t = slab_rows(rows, w_gate)
        up_t = slab_rows(rows, w_up)
        hidden = (jax.nn.silu(gate_t) * up_t).astype(jnp.bfloat16)
        return jnp.dot(hidden, w_down, preferred_element_type=jnp.float32).astype(jnp.bfloat16)

    def grad_block(index):
        owner = (index - 1) % N_BLK
        gate_slab = pick(gate_slabs, owner)
        up_slab = pick(up_slabs, owner)
        down_slab = pick(down_slabs, owner)
        acc_gate = jnp.zeros((SLAB, D), jnp.float32)
        acc_up = jnp.zeros((SLAB, D), jnp.float32)
        acc_down = jnp.zeros((SLAB, D), jnp.float32)
        for step in range(BWD_STEPS):
            source = (owner + step) % N_BLK
            parts = grad_term(pick(blocks, source), pick(grad_blocks, source), gate_slab, up_slab, down_slab)
            acc_gate = acc_gate + parts[0]
            acc_up = acc_up + parts[1]
            acc_down = acc_down + parts[2]
        return acc_gate, acc_up, acc_down

    mixed = lax.map(forward_block, blocks).reshape(TOKENS, D)
    indices = jnp.arange(N_BLK, dtype=jnp.int32)
    grad_gate, grad_up, grad_down = lax.map(grad_block, indices)
    return mixed, grad_gate.reshape(FF, D), grad_up.reshape(FF, D), grad_down.reshape(FF, D)
```

```python
import jax
import jax.numpy as jnp
from jax import lax
from jax.sharding import PartitionSpec as P

BF = jnp.bfloat16
F32 = jnp.float32


def shifted(array, axis, by):
    count = lax.axis_size(axis)
    return lax.ppermute(array, axis, [(i, (i + by) % count) for i in range(count)])


def nt(a, b):
    return lax.dot_general(a, b, (((1,), (1,)), ((), ())), preferred_element_type=F32)


def tn(a, b):
    return lax.dot_general(a, b, (((0,), (0,)), ((), ())), preferred_element_type=F32)


def on_device(tokens, out_grad, w_gate, w_up, w_down):
    n = lax.axis_size("blk")
    b = lax.axis_index("blk")
    rows = tokens.shape[0]

    y_prev = shifted(out_grad, "blk", 1)
    y_next = shifted(out_grad, "blk", -1)
    x_cols = lax.all_gather(tokens, "blk", axis=0, tiled=True)
    x = lax.all_gather(x_cols, "inner", axis=1, tiled=True)
    y = lax.all_gather(
        jnp.concatenate([y_prev, out_grad, y_next], axis=0), "inner", axis=1, tiled=True
    )

    def block(array, index):
        return lax.dynamic_slice_in_dim(array, (index % n) * rows, rows, 0)

    def pair(array, first):
        return jnp.concatenate([block(array, first), block(array, first + 1)], axis=0)

    gate = nt(x, w_gate)
    up = nt(x, w_up)
    hidden = (jax.nn.silu(gate) * up).astype(BF)

    gate_2 = pair(gate, b)
    up_2 = pair(up, b)
    hidden_2 = pair(hidden, b)
    back = nt(y[rows:], w_down)
    sigma = jax.nn.sigmoid(gate_2)
    dgate = (back * up_2 * sigma * (1.0 + gate_2 * (1.0 - sigma))).astype(BF)
    dup = (back * gate_2 * sigma).astype(BF)
    moved = shifted(jnp.stack([dgate, dup, hidden_2]), "blk", 1)

    partial = jnp.dot(hidden, w_down, preferred_element_type=F32).astype(BF)
    mixed = lax.psum_scatter(partial, "inner", scatter_dimension=1, tiled=True)
    mixed = lax.psum_scatter(mixed, "blk", scatter_dimension=0, tiled=True).astype(BF)

    x_2 = pair(x, b - 1 + n)
    y_2 = y[: 2 * rows]
    return (mixed, tn(moved[0], x_2), tn(moved[1], x_2), tn(moved[2], y_2))


def solution(mesh):
    return jax.shard_map(
        on_device,
        mesh=mesh,
        in_specs=(
            P(("groups", "blk"), "inner"),
            P(("groups", "blk"), "inner"),
            P(("blk", "inner"), None),
            P(("blk", "inner"), None),
            P(("blk", "inner"), None),
        ),
        out_specs=(
            P(("groups", "blk"), "inner"),
            P(("groups", "blk", "inner"), None),
            P(("groups", "blk", "inner"), None),
            P(("groups", "blk", "inner"), None),
        ),
        check_vma=False,
    )
```

```python
import functools

import jax
import jax.numpy as jnp
from jax import lax
from jax.experimental import pallas as pl
from jax.experimental.pallas import tpu as pltpu
from jax.sharding import PartitionSpec as P

BF = jnp.bfloat16
F32 = jnp.float32


def shifted(array, axis, by):
    count = lax.axis_size(axis)
    return lax.ppermute(array, axis, [(i, (i + by) % count) for i in range(count)])


def nt(a, b):
    return lax.dot_general(a, b, (((1,), (1,)), ((), ())), preferred_element_type=F32)


def tn(a, b):
    return lax.dot_general(a, b, (((0,), (0,)), ((), ())), preferred_element_type=F32)


def on_device(tokens, out_grad, w_gate, w_up, w_down):
    n = lax.axis_size("blk")
    b = lax.axis_index("blk")
    rows = tokens.shape[0]

    y_prev = shifted(out_grad, "blk", 1)
    y_next = shifted(out_grad, "blk", -1)
    x_cols = lax.all_gather(tokens, "blk", axis=0, tiled=True)
    x = lax.all_gather(x_cols, "inner", axis=1, tiled=True)
    y = lax.all_gather(
        jnp.concatenate([y_prev, out_grad, y_next], axis=0), "inner", axis=1, tiled=True
    )

    def block(array, index):
        return lax.dynamic_slice_in_dim(array, (index % n) * rows, rows, 0)

    def pair(array, first):
        return jnp.concatenate([block(array, first), block(array, first + 1)], axis=0)

    gate = nt(x, w_gate)
    up = nt(x, w_up)
    hidden = (jax.nn.silu(gate) * up).astype(BF)

    gate_2 = pair(gate, b)
    up_2 = pair(up, b)
    hidden_2 = pair(hidden, b)
    back = nt(y[rows:], w_down)
    sigma = jax.nn.sigmoid(gate_2)
    dgate = (back * up_2 * sigma * (1.0 + gate_2 * (1.0 - sigma))).astype(BF)
    dup = (back * gate_2 * sigma).astype(BF)
    moved = shifted(jnp.stack([dgate, dup, hidden_2]), "blk", 1)

    partial = jnp.dot(hidden, w_down, preferred_element_type=F32).astype(BF)
    mixed = lax.psum_scatter(partial, "inner", scatter_dimension=1, tiled=True)
    mixed = lax.psum_scatter(mixed, "blk", scatter_dimension=0, tiled=True).astype(BF)

    x_2 = pair(x, b - 1 + n)
    y_2 = y[: 2 * rows]
    return (mixed, tn(moved[0], x_2), tn(moved[1], x_2), tn(moved[2], y_2))


MESH = pl.DeviceIdType.MESH


def places():
    z = lax.axis_index("blk")
    i = lax.axis_index("inner")
    x, c = i // 2, lax.rem(i, 2)
    return z, i, (1 - x) * 2 + c, x * 2 + (1 - c), (1 - x) * 2 + (1 - c)


def greet(z, i, n, ix, ic):
    barrier = pltpu.get_barrier_semaphore()
    for k in range(1, n):
        pl.semaphore_signal(
            barrier, inc=1, device_id={"blk": lax.rem(z + k, n), "inner": i}, device_id_type=MESH
        )
    for other in (ix, ic):
        pl.semaphore_signal(
            barrier, inc=1, device_id={"blk": z, "inner": other}, device_id_type=MESH
        )
    pl.semaphore_wait(barrier, n + 1)


def gather_kernel(n, t_ref, g_ref, x_ref, y_ref, zsend, send, recv):
    z, i, ix, ic, ixc = places()
    cols = t_ref.shape[1]

    def view(item, inner):
        ref, slot, _ = item
        return ref.at[slot, :, pl.ds(pl.multiple_of(inner * cols, cols), cols)]

    def copy(src, dst, ssem, rsem, blk, inner):
        return pltpu.make_async_remote_copy(
            src_ref=src, dst_ref=dst, send_sem=ssem, recv_sem=rsem,
            device_id={"blk": blk, "inner": inner}, device_id_type=MESH,
        )

    greet(z, i, n, ix, ic)

    def x_item(k):
        slot = lax.rem(z + k, n)
        return (x_ref, slot, slot)

    def y_item(slot):
        return (y_ref, slot, n + slot)

    own_x, own_y = x_item(0), y_item(1)
    z_copies = []

    def z_send(src, item, blk):
        q = item[2]
        made = copy(src, view(item, i), zsend.at[len(z_copies)], recv.at[q, 0], blk, i)
        made.start()
        z_copies.append(made)

    up, down = lax.rem(z + 1, n), lax.rem(z + n - 1, n)
    z_send(t_ref, own_x, up)
    z_send(t_ref, own_x, down)
    for k in range(2, n - 1):
        z_send(t_ref, own_x, lax.rem(z + k, n))
    z_send(g_ref, y_item(2), down)
    z_send(g_ref, y_item(0), up)
    here = pl.ds(pl.multiple_of(i * cols, cols), cols)
    x_ref[z, :, here] = t_ref[...]
    y_ref[1, :, here] = g_ref[...]

    items = [own_x, own_y, x_item(1), x_item(n - 1), y_item(2)]
    items += [x_item(k) for k in range(2, n - 1)] + [y_item(0)]
    sent = []

    def second(item):
        q = item[2]
        v = view(item, ix)
        copy(v, v, send.at[q, 1], recv.at[q, 1], z, ix).wait_recv()
        made = copy(v, v, send.at[q, 2], recv.at[q, 3], z, ic)
        made.start()
        sent.append(made)

    for at, item in enumerate(items):
        q = item[2]
        v = view(item, i)
        if at >= 2:
            copy(v, v, send.at[q, 0], recv.at[q, 0], z, ix).wait_recv()
        made = copy(v, v, send.at[q, 0], recv.at[q, 1], z, ix)
        made.start()
        sent.append(made)
        made = copy(v, v, send.at[q, 1], recv.at[q, 2], z, ic)
        made.start()
        sent.append(made)
        if at >= 1:
            second(items[at - 1])
    second(items[-1])
    for item in items:
        q = item[2]
        v = view(item, ic)
        copy(v, v, send.at[q, 1], recv.at[q, 2], z, ic).wait_recv()
        v = view(item, ixc)
        copy(v, v, send.at[q, 2], recv.at[q, 3], z, ic).wait_recv()
    for made in z_copies + sent:
        made.wait_send()


def gather(n, m, tokens, out_grad):
    rows, cols = tokens.shape
    vmem = pl.BlockSpec(memory_space=pltpu.VMEM)
    return pl.pallas_call(
        functools.partial(gather_kernel, n),
        out_shape=(
            jax.ShapeDtypeStruct((n, rows, m * cols), BF),
            jax.ShapeDtypeStruct((3, rows, m * cols), BF),
        ),
        in_specs=[vmem, vmem],
        out_specs=(vmem, vmem),
        scratch_shapes=[
            pltpu.SemaphoreType.DMA((n + 1,)),
            pltpu.SemaphoreType.DMA((n + 3, 3)),
            pltpu.SemaphoreType.DMA((n + 3, 4)),
        ],
        compiler_params=pltpu.CompilerParams(
            collective_id=0, has_side_effects=True, vmem_limit_bytes=32 * 1024 * 1024
        ),
    )(tokens, out_grad)


def scatter_kernel(
    n, h_ref, w_ref, out_ref, own, oth, a_out, a_in, b_out, b_in, c_out, c_in, send, recv
):
    z, i, ix, ic, ixc = places()
    x = i // 2
    cols = out_ref.shape[1]
    order = [k for k in range(2, n - 1)] + [1, n - 1, 0]

    def copy(src, dst, stage, k, blk, inner):
        return pltpu.make_async_remote_copy(
            src_ref=src, dst_ref=dst, send_sem=send.at[stage, k], recv_sem=recv.at[stage, k],
            device_id={"blk": blk, "inner": inner}, device_id_type=MESH,
        )

    greet(z, i, n, ix, ic)

    def share(k, inner):
        return jnp.dot(
            h_ref[lax.rem(z + k, n)],
            w_ref[:, pl.ds(pl.multiple_of(inner * cols, cols), cols)],
            preferred_element_type=F32,
        )

    sent = []

    def go(made):
        made.start()
        sent.append(made)

    for k in order:
        a_out[k, 0] = share(k, ixc).astype(BF)
        a_out[k, 1] = share(k, ic).astype(BF)
        go(copy(a_out.at[k], a_in.at[k], 0, k, z, ic))
        oth[k] = share(k, ix)
        own[k] = share(k, i)
    for k in order:
        copy(a_out.at[k], a_in.at[k], 0, k, z, ic).wait_recv()
        b_out[k] = (oth[k] + a_in[k, 0].astype(F32)).astype(BF)
        go(copy(b_out.at[k], b_in.at[k], 1, k, z, ix))
    for k in order:
        copy(b_out.at[k], b_in.at[k], 1, k, z, ix).wait_recv()
        total = own[k] + a_in[k, 1].astype(F32) + b_in[k].astype(F32)
        if k:
            c_out[k] = total.astype(BF)
            go(copy(c_out.at[k], c_in.at[k], 2, k, lax.rem(z + k, n), i))
    for k in range(1, n):
        copy(c_out.at[k], c_in.at[k], 2, k, lax.rem(z + k, n), i).wait_recv()
        total = total + c_in[k].astype(F32)
    out_ref[...] = total.astype(BF)
    for made in sent:
        made.wait_send()


def scatter(n, m, hidden, w_down):
    _, rows, _ = hidden.shape
    cols = w_down.shape[1] // m
    vmem = pl.BlockSpec(memory_space=pltpu.VMEM)
    return pl.pallas_call(
        functools.partial(scatter_kernel, n),
        out_shape=jax.ShapeDtypeStruct((rows, cols), BF),
        in_specs=[vmem, vmem],
        out_specs=vmem,
        scratch_shapes=[
            pltpu.VMEM((n, rows, cols), F32),
            pltpu.VMEM((n, rows, cols), F32),
            pltpu.VMEM((n, 2, rows, cols), BF),
            pltpu.VMEM((n, 2, rows, cols), BF),
            pltpu.VMEM((n, rows, cols), BF),
            pltpu.VMEM((n, rows, cols), BF),
            pltpu.VMEM((n, rows, cols), BF),
            pltpu.VMEM((n, rows, cols), BF),
            pltpu.SemaphoreType.DMA((3, n)),
            pltpu.SemaphoreType.DMA((3, n)),
        ],
        compiler_params=pltpu.CompilerParams(
            collective_id=1, has_side_effects=True, vmem_limit_bytes=32 * 1024 * 1024
        ),
    )(hidden, w_down)


def on_square(tokens, out_grad, w_gate, w_up, w_down):
    n, m = lax.axis_size("blk"), lax.axis_size("inner")
    b = lax.axis_index("blk")
    rows = tokens.shape[0]
    units, width = w_gate.shape

    x, y = gather(n, m, tokens, out_grad)

    def pair(array, first):
        return jnp.concatenate(
            [lax.dynamic_index_in_dim(array, (first + j) % n, 0, keepdims=False) for j in (0, 1)], 0
        )

    flat = x.reshape(n * rows, width)
    gate = nt(flat, w_gate)
    up = nt(flat, w_up)
    hidden = (jax.nn.silu(gate) * up).astype(BF).reshape(n, rows, units)

    gate_2 = pair(gate.reshape(n, rows, units), b)
    up_2 = pair(up.reshape(n, rows, units), b)
    hidden_2 = pair(hidden, b)
    back = nt(y[1:].reshape(2 * rows, width), w_down)
    sigma = jax.nn.sigmoid(gate_2)
    dgate = (back * up_2 * sigma * (1.0 + gate_2 * (1.0 - sigma))).astype(BF)
    dup = (back * gate_2 * sigma).astype(BF)
    moved = [shifted(part, "blk", 1) for part in (hidden_2, dgate, dup)]
    mixed = scatter(n, m, hidden, w_down)

    x_2 = pair(x, b - 1 + n)
    y_2 = y[:2].reshape(2 * rows, width)
    return (mixed, tn(moved[1], x_2), tn(moved[2], x_2), tn(moved[0], y_2))


def solution(mesh):
    square = mesh.shape["inner"] == 4 and mesh.shape["blk"] == 4
    return jax.shard_map(
        on_square if square else on_device,
        mesh=mesh,
        in_specs=(
            P(("groups", "blk"), "inner"),
            P(("groups", "blk"), "inner"),
            P(("blk", "inner"), None),
            P(("blk", "inner"), None),
            P(("blk", "inner"), None),
        ),
        out_specs=(
            P(("groups", "blk"), "inner"),
            P(("groups", "blk", "inner"), None),
            P(("groups", "blk", "inner"), None),
            P(("groups", "blk", "inner"), None),
        ),
        check_vma=False,
    )
```

```python
import functools

import jax
import jax.numpy as jnp
from jax import lax
from jax.experimental import pallas as pl
from jax.experimental.pallas import tpu as pltpu
from jax.sharding import PartitionSpec as P

BF = jnp.bfloat16
F32 = jnp.float32


def shifted(array, axis, by):
    count = lax.axis_size(axis)
    return lax.ppermute(array, axis, [(i, (i + by) % count) for i in range(count)])


def nt(a, b):
    return lax.dot_general(a, b, (((1,), (1,)), ((), ())), preferred_element_type=F32)


def tn(a, b):
    return lax.dot_general(a, b, (((0,), (0,)), ((), ())), preferred_element_type=F32)


def on_device(tokens, out_grad, w_gate, w_up, w_down):
    n = lax.axis_size("blk")
    b = lax.axis_index("blk")
    rows = tokens.shape[0]

    y_prev = shifted(out_grad, "blk", 1)
    y_next = shifted(out_grad, "blk", -1)
    x_cols = lax.all_gather(tokens, "blk", axis=0, tiled=True)
    x = lax.all_gather(x_cols, "inner", axis=1, tiled=True)
    y = lax.all_gather(
        jnp.concatenate([y_prev, out_grad, y_next], axis=0), "inner", axis=1, tiled=True
    )

    def block(array, index):
        return lax.dynamic_slice_in_dim(array, (index % n) * rows, rows, 0)

    def pair(array, first):
        return jnp.concatenate([block(array, first), block(array, first + 1)], axis=0)

    gate = nt(x, w_gate)
    up = nt(x, w_up)
    hidden = (jax.nn.silu(gate) * up).astype(BF)

    gate_2 = pair(gate, b)
    up_2 = pair(up, b)
    hidden_2 = pair(hidden, b)
    back = nt(y[rows:], w_down)
    sigma = jax.nn.sigmoid(gate_2)
    dgate = (back * up_2 * sigma * (1.0 + gate_2 * (1.0 - sigma))).astype(BF)
    dup = (back * gate_2 * sigma).astype(BF)
    moved = shifted(jnp.stack([dgate, dup, hidden_2]), "blk", 1)

    partial = jnp.dot(hidden, w_down, preferred_element_type=F32).astype(BF)
    mixed = lax.psum_scatter(partial, "inner", scatter_dimension=1, tiled=True)
    mixed = lax.psum_scatter(mixed, "blk", scatter_dimension=0, tiled=True).astype(BF)

    x_2 = pair(x, b - 1 + n)
    y_2 = y[: 2 * rows]
    return (mixed, tn(moved[0], x_2), tn(moved[1], x_2), tn(moved[2], y_2))


MESH = pl.DeviceIdType.MESH


def remote(src, dst, ssem, rsem, blk, inner):
    return pltpu.make_async_remote_copy(
        src_ref=src, dst_ref=dst, send_sem=ssem, recv_sem=rsem,
        device_id={"blk": blk, "inner": inner}, device_id_type=MESH,
    )


def greet(z, i, n, ix, ic):
    barrier = pltpu.get_barrier_semaphore()
    for k in range(1, n):
        pl.semaphore_signal(
            barrier, inc=1, device_id={"blk": lax.rem(z + k, n), "inner": i}, device_id_type=MESH
        )
    for other in (ix, ic):
        pl.semaphore_signal(
            barrier, inc=1, device_id={"blk": z, "inner": other}, device_id_type=MESH
        )
    pl.semaphore_wait(barrier, n + 1)


def step_kernel(
    n, t_ref, g_ref, wg_hbm, wu_hbm, wd_hbm,
    x_out, y_out, m_in, c_out, own_out,
    x_rest, y_next, wg, wu, wd, hid, m_out, own, oth, a_out, a_in, b_out, b_in,
    local, zsend, send, recv, msend, mrecv, rsend, rrecv,
):
    z, i = lax.axis_index("blk"), lax.axis_index("inner")
    x, c = i // 2, lax.rem(i, 2)
    ix, ic, ixc = (1 - x) * 2 + c, x * 2 + (1 - c), (1 - x) * 2 + (1 - c)
    rows, cols = t_ref.shape
    units = hid.shape[2]

    def part(inner):
        return pl.ds(pl.multiple_of(inner * cols, cols), cols)

    def block(q):
        if q < n:
            return x_out.at[q] if q < 2 else x_rest.at[q - 2]
        return y_out.at[q - n] if q < n + 2 else y_next.at[0]

    def view(q, inner):
        return block(q).at[:, part(inner)]

    loads = [
        pltpu.make_async_copy(wg_hbm, wg, local.at[0]),
        pltpu.make_async_copy(wu_hbm, wu, local.at[1]),
        pltpu.make_async_copy(wd_hbm, wd, local.at[2]),
        pltpu.make_async_copy(t_ref, view(1, i), local.at[3]),
        pltpu.make_async_copy(g_ref, view(n + 1, i), local.at[4]),
    ]
    for load in (loads[3], loads[4], loads[0], loads[1], loads[2]):
        load.start()
    greet(z, i, n, ix, ic)

    sent = []

    def go(made):
        made.start()
        sent.append(made)

    def first(q):
        src = view(q, i)
        if q == 1:
            src = t_ref
        elif q == n + 1:
            src = g_ref
        else:
            remote(src, src, send.at[q, 0], recv.at[q, 0], z, ix).wait_recv()
        go(remote(src, view(q, i), send.at[q, 0], recv.at[q, 1], z, ix))
        go(remote(src, view(q, i), send.at[q, 1], recv.at[q, 2], z, ic))

    def second(q):
        v = view(q, ix)
        remote(v, v, send.at[q, 1], recv.at[q, 1], z, ix).wait_recv()
        go(remote(v, v, send.at[q, 2], recv.at[q, 3], z, ic))

    def whole(q):
        for inner, sem in ((ic, 2), (ixc, 3)):
            v = view(q, inner)
            remote(v, v, send.at[q, 1], recv.at[q, sem], z, ic).wait_recv()

    def z_send(src, q, k, at):
        go(remote(src, view(q, i), zsend.at[at], recv.at[q, 0], lax.rem(z + k, n), i))

    def forward(s):
        half = units // 2
        for u in range(2):
            span = pl.ds(u * half, half)
            rows_x = block(s)[...]
            gate = nt(rows_x, wg[span, :])
            up = nt(rows_x, wu[span, :])
            sigma = jax.nn.sigmoid(gate)
            active = gate * sigma
            hidden = (active * up).astype(BF)
            hid[s, :, span] = hidden
            if s in (1, 2):
                back = nt(block(n + s)[...], wd[span, :])
                m_out[s - 1, 0, :, span] = (
                    back * up * sigma * (1.0 + gate * (1.0 - sigma))
                ).astype(BF)
                m_out[s - 1, 1, :, span] = (back * active).astype(BF)
                m_out[s - 1, 2, :, span] = hidden
        if s in (1, 2):
            go(m_copy(s - 1))

    def m_copy(j):
        return remote(
            m_out.at[j], m_in.at[:, pl.ds(j * rows, rows), :],
            msend.at[j], mrecv.at[j], lax.rem(z + 1, n), i,
        )

    def share(s, inner):
        return jnp.dot(hid[s], wd[:, part(inner)], preferred_element_type=F32)

    def a_copy(s):
        return remote(a_out.at[s], a_in.at[s], rsend.at[0, s], rrecv.at[0, s], z, ic)

    def b_copy(s):
        return remote(b_out.at[s], b_in.at[s], rsend.at[1, s], rrecv.at[1, s], z, ix)

    def stage_a(s):
        a_out[s, 0] = share(s, ixc).astype(BF)
        a_out[s, 1] = share(s, ic).astype(BF)
        go(a_copy(s))
        oth[s] = share(s, ix)
        own[s] = share(s, i)

    def stage_b(s):
        a_copy(s).wait_recv()
        b_out[s] = (oth[s] + a_in[s, 0].astype(F32)).astype(BF)
        go(b_copy(s))

    def stage_c(s):
        b_copy(s).wait_recv()
        total = own[s] + a_in[s, 1].astype(F32) + b_in[s].astype(F32)
        if s == 1:
            own_out[...] = total
        else:
            c_out[s if s == 0 else s - 1] = total.astype(BF)

    first(1)
    first(n + 1)
    z_send(t_ref, 0, 1, 0)
    z_send(t_ref, 2, n - 1, 1)
    z_send(g_ref, n + 2, n - 1, 2)
    for k in range(2, n - 1):
        z_send(t_ref, n - k + 1, k, 2 + k)
    z_send(g_ref, n, 1, 3)
    second(1)
    second(n + 1)
    first(2)
    first(n + 2)
    for load in loads:
        load.wait()
    whole(1)
    whole(n + 1)
    forward(1)
    first(0)
    second(2)
    second(n + 2)
    stage_a(1)
    whole(2)
    whole(n + 2)
    forward(2)
    for s in range(3, n):
        first(s)
    second(0)
    stage_a(2)
    stage_b(2)
    whole(0)
    forward(0)
    for s in range(3, n):
        second(s)
    stage_a(0)
    stage_b(0)
    first(n)
    for s in range(3, n):
        whole(s)
        forward(s)
        stage_a(s)
        stage_b(s)
    stage_b(1)
    second(n)
    stage_c(2)
    stage_c(0)
    for s in range(3, n):
        stage_c(s)
    stage_c(1)
    whole(n)
    for j in range(2):
        m_copy(j).wait_recv()
    for made in sent:
        made.wait_send()


def on_square(tokens, out_grad, w_gate, w_up, w_down):
    n, m = lax.axis_size("blk"), lax.axis_size("inner")
    rows, cols = tokens.shape
    units, width = w_gate.shape
    vmem = pl.BlockSpec(memory_space=pltpu.VMEM)
    hbm = pl.BlockSpec(memory_space=pl.ANY)
    dma = pltpu.SemaphoreType.DMA
    x, y, moved, parts, total = pl.pallas_call(
        functools.partial(step_kernel, n),
        out_shape=(
            jax.ShapeDtypeStruct((2, rows, width), BF),
            jax.ShapeDtypeStruct((2, rows, width), BF),
            jax.ShapeDtypeStruct((3, 2 * rows, units), BF),
            jax.ShapeDtypeStruct((n - 1, rows, cols), BF),
            jax.ShapeDtypeStruct((rows, cols), F32),
        ),
        in_specs=[hbm] * 5,
        out_specs=(vmem,) * 5,
        scratch_shapes=[
            pltpu.VMEM((n - 2, rows, width), BF),
            pltpu.VMEM((1, rows, width), BF),
            pltpu.VMEM((units, width), BF),
            pltpu.VMEM((units, width), BF),
            pltpu.VMEM((units, width), BF),
            pltpu.VMEM((n, rows, units), BF),
            pltpu.VMEM((2, 3, rows, units), BF),
            pltpu.VMEM((n, rows, cols), F32),
            pltpu.VMEM((n, rows, cols), F32),
            pltpu.VMEM((n, 2, rows, cols), BF),
            pltpu.VMEM((n, 2, rows, cols), BF),
            pltpu.VMEM((n, rows, cols), BF),
            pltpu.VMEM((n, rows, cols), BF),
            dma((5,)),
            dma((n + 1,)),
            dma((n + 3, 3)),
            dma((n + 3, 4)),
            dma((2,)),
            dma((2,)),
            dma((2, n)),
            dma((2, n)),
        ],
        compiler_params=pltpu.CompilerParams(
            collective_id=0, has_side_effects=True, vmem_limit_bytes=56 * 1024 * 1024
        ),
    )(tokens, out_grad, w_gate, w_up, w_down)

    for at, by in enumerate([-1] + list(range(1, n - 1))):
        total = total + shifted(parts[at], "blk", by).astype(F32)
    x_2 = x.reshape(2 * rows, width)
    y_2 = y.reshape(2 * rows, width)
    return (total.astype(BF), tn(moved[0], x_2), tn(moved[1], x_2), tn(moved[2], y_2))


def solution(mesh):
    square = mesh.shape["inner"] == 4 and mesh.shape["blk"] == 4
    return jax.shard_map(
        on_square if square else on_device,
        mesh=mesh,
        in_specs=(
            P(("groups", "blk"), "inner"),
            P(("groups", "blk"), "inner"),
            P(("blk", "inner"), None),
            P(("blk", "inner"), None),
            P(("blk", "inner"), None),
        ),
        out_specs=(
            P(("groups", "blk"), "inner"),
            P(("groups", "blk", "inner"), None),
            P(("groups", "blk", "inner"), None),
            P(("groups", "blk", "inner"), None),
        ),
        check_vma=False,
    )
```

```python
import functools

import jax
import jax.numpy as jnp
from jax import lax
from jax.experimental import pallas as pl
from jax.experimental.pallas import tpu as pltpu
from jax.sharding import PartitionSpec as P

BF = jnp.bfloat16
F32 = jnp.float32


def shifted(array, axis, by):
    count = lax.axis_size(axis)
    return lax.ppermute(array, axis, [(i, (i + by) % count) for i in range(count)])


def nt(a, b):
    return lax.dot_general(a, b, (((1,), (1,)), ((), ())), preferred_element_type=F32)


def tn(a, b):
    return lax.dot_general(a, b, (((0,), (0,)), ((), ())), preferred_element_type=F32)


def on_device(tokens, out_grad, w_gate, w_up, w_down):
    n = lax.axis_size("blk")
    b = lax.axis_index("blk")
    rows = tokens.shape[0]

    y_prev = shifted(out_grad, "blk", 1)
    y_next = shifted(out_grad, "blk", -1)
    x_cols = lax.all_gather(tokens, "blk", axis=0, tiled=True)
    x = lax.all_gather(x_cols, "inner", axis=1, tiled=True)
    y = lax.all_gather(
        jnp.concatenate([y_prev, out_grad, y_next], axis=0), "inner", axis=1, tiled=True
    )

    def block(array, index):
        return lax.dynamic_slice_in_dim(array, (index % n) * rows, rows, 0)

    def pair(array, first):
        return jnp.concatenate([block(array, first), block(array, first + 1)], axis=0)

    gate = nt(x, w_gate)
    up = nt(x, w_up)
    hidden = (jax.nn.silu(gate) * up).astype(BF)

    gate_2 = pair(gate, b)
    up_2 = pair(up, b)
    hidden_2 = pair(hidden, b)
    back = nt(y[rows:], w_down)
    sigma = jax.nn.sigmoid(gate_2)
    dgate = (back * up_2 * sigma * (1.0 + gate_2 * (1.0 - sigma))).astype(BF)
    dup = (back * gate_2 * sigma).astype(BF)
    moved = shifted(jnp.stack([dgate, dup, hidden_2]), "blk", 1)

    partial = jnp.dot(hidden, w_down, preferred_element_type=F32).astype(BF)
    mixed = lax.psum_scatter(partial, "inner", scatter_dimension=1, tiled=True)
    mixed = lax.psum_scatter(mixed, "blk", scatter_dimension=0, tiled=True).astype(BF)

    x_2 = pair(x, b - 1 + n)
    y_2 = y[: 2 * rows]
    return (mixed, tn(moved[0], x_2), tn(moved[1], x_2), tn(moved[2], y_2))


MESH = pl.DeviceIdType.MESH


def remote(src, dst, ssem, rsem, blk, inner):
    return pltpu.make_async_remote_copy(
        src_ref=src, dst_ref=dst, send_sem=ssem, recv_sem=rsem,
        device_id={"blk": blk, "inner": inner}, device_id_type=MESH,
    )


def greet(z, i, n, ix, ic):
    barrier = pltpu.get_barrier_semaphore()
    for k in range(1, n):
        pl.semaphore_signal(
            barrier, inc=1, device_id={"blk": lax.rem(z + k, n), "inner": i}, device_id_type=MESH
        )
    for other in (ix, ic):
        pl.semaphore_signal(
            barrier, inc=1, device_id={"blk": z, "inner": other}, device_id_type=MESH
        )
    pl.semaphore_wait(barrier, n + 1)


def step_kernel(
    n, t_ref, g_ref, wg_hbm, wu_hbm, wd_hbm,
    x_out, y_out, m_in, c_out, own_out,
    x_rest, y_next, wg, wu, wd, hid, m_out, own, oth, a_out, a_in, b_out, b_in,
    local, zsend, send, recv, msend, mrecv, rsend, rrecv,
):
    z, i = lax.axis_index("blk"), lax.axis_index("inner")
    x, c = i // 2, lax.rem(i, 2)
    ix, ic, ixc = (1 - x) * 2 + c, x * 2 + (1 - c), (1 - x) * 2 + (1 - c)
    rows, cols = t_ref.shape
    units = hid.shape[2]

    def part(inner):
        return pl.ds(pl.multiple_of(inner * cols, cols), cols)

    def block(q):
        if q < n:
            return x_out.at[q] if q < 2 else x_rest.at[q - 2]
        return y_out.at[q - n] if q < n + 2 else y_next.at[0]

    def view(q, inner):
        return block(q).at[:, part(inner)]

    loads = [
        pltpu.make_async_copy(wg_hbm, wg, local.at[0]),
        pltpu.make_async_copy(wu_hbm, wu, local.at[1]),
        pltpu.make_async_copy(wd_hbm, wd, local.at[2]),
        pltpu.make_async_copy(t_ref, view(1, i), local.at[3]),
        pltpu.make_async_copy(g_ref, view(n + 1, i), local.at[4]),
    ]
    for load in (loads[3], loads[4], loads[0], loads[1], loads[2]):
        load.start()
    greet(z, i, n, ix, ic)

    sent = []

    def go(made):
        made.start()
        sent.append(made)

    def first(q):
        src = view(q, i)
        if q == 1:
            src = t_ref
        elif q == n + 1:
            src = g_ref
        else:
            remote(src, src, send.at[q, 0], recv.at[q, 0], z, ix).wait_recv()
        go(remote(src, view(q, i), send.at[q, 0], recv.at[q, 1], z, ix))
        go(remote(src, view(q, i), send.at[q, 1], recv.at[q, 2], z, ic))

    def second(q):
        v = view(q, ix)
        remote(v, v, send.at[q, 1], recv.at[q, 1], z, ix).wait_recv()
        go(remote(v, v, send.at[q, 2], recv.at[q, 3], z, ic))

    def whole(q):
        for inner, sem in ((ic, 2), (ixc, 3)):
            v = view(q, inner)
            remote(v, v, send.at[q, 1], recv.at[q, sem], z, ic).wait_recv()

    def z_copy(src, q, k, at):
        return remote(src, view(q, i), zsend.at[at], recv.at[q, 0], lax.rem(z + k, n), i)

    def forward(s):
        half = units // 2
        for u in range(2):
            span = pl.ds(u * half, half)
            rows_x = block(s)[...]
            gate = nt(rows_x, wg[span, :])
            up = nt(rows_x, wu[span, :])
            sigma = jax.nn.sigmoid(gate)
            active = gate * sigma
            hidden = (active * up).astype(BF)
            hid[s, :, span] = hidden
            if s in (1, 2):
                back = nt(block(n + s)[...], wd[span, :])
                m_out[s - 1, 0, :, span] = (
                    back * up * sigma * (1.0 + gate * (1.0 - sigma))
                ).astype(BF)
                m_out[s - 1, 1, :, span] = (back * active).astype(BF)
                m_out[s - 1, 2, :, span] = hidden
        if s in (1, 2):
            go(m_copy(s - 1))

    def m_copy(j):
        return remote(
            m_out.at[j], m_in.at[:, pl.ds(j * rows, rows), :],
            msend.at[j], mrecv.at[j], lax.rem(z + 1, n), i,
        )

    def share(s, inner):
        return jnp.dot(hid[s], wd[:, part(inner)], preferred_element_type=F32)

    def a_copy(s):
        return remote(a_out.at[s], a_in.at[s], rsend.at[0, s], rrecv.at[0, s], z, ic)

    def b_copy(s):
        return remote(b_out.at[s], b_in.at[s], rsend.at[1, s], rrecv.at[1, s], z, ix)

    def stage_a(s):
        a_out[s, 0] = share(s, ixc).astype(BF)
        a_out[s, 1] = share(s, ic).astype(BF)
        go(a_copy(s))
        oth[s] = share(s, ix)
        own[s] = share(s, i)

    def stage_b(s):
        a_copy(s).wait_recv()
        b_out[s] = (oth[s] + a_in[s, 0].astype(F32)).astype(BF)
        go(b_copy(s))

    def stage_c(s):
        b_copy(s).wait_recv()
        total = own[s] + a_in[s, 1].astype(F32) + b_in[s].astype(F32)
        if s == 1:
            own_out[...] = total
        else:
            c_out[s if s == 0 else s - 1] = total.astype(BF)

    first(1)
    first(n + 1)
    ups = [z_copy(t_ref, 0, 1, 0), z_copy(g_ref, n, 1, 3)]
    downs = [z_copy(t_ref, 2, n - 1, 1), z_copy(g_ref, n + 2, n - 1, 2)]
    fars = [z_copy(t_ref, n - k + 1, k, 2 + k) for k in range(2, n - 1)]

    @pl.when(z == 0)
    def _():
        for made in ups + fars + downs:
            made.start()

    @pl.when(z == n - 1)
    def _():
        for made in downs + fars + ups:
            made.start()

    @pl.when((z > 0) & (z < n - 1))
    def _():
        for made in [ups[0]] + downs + fars + [ups[1]]:
            made.start()

    sent.extend(ups + downs + fars)
    second(1)
    second(n + 1)
    first(2)
    first(n + 2)
    for load in loads:
        load.wait()
    whole(1)
    whole(n + 1)
    forward(1)
    first(0)
    second(2)
    second(n + 2)
    stage_a(1)
    whole(2)
    whole(n + 2)
    forward(2)
    for s in range(3, n):
        first(s)
    second(0)
    stage_a(2)
    stage_b(2)
    whole(0)
    forward(0)
    for s in range(3, n):
        second(s)
    stage_a(0)
    stage_b(0)
    first(n)
    for s in range(3, n):
        whole(s)
        forward(s)
        stage_a(s)
        stage_b(s)
    stage_b(1)
    second(n)
    stage_c(2)
    stage_c(0)
    for s in range(3, n):
        stage_c(s)
    stage_c(1)
    whole(n)
    for j in range(2):
        m_copy(j).wait_recv()
    for made in sent:
        made.wait_send()


def on_square(tokens, out_grad, w_gate, w_up, w_down):
    n, m = lax.axis_size("blk"), lax.axis_size("inner")
    rows, cols = tokens.shape
    units, width = w_gate.shape
    vmem = pl.BlockSpec(memory_space=pltpu.VMEM)
    hbm = pl.BlockSpec(memory_space=pl.ANY)
    dma = pltpu.SemaphoreType.DMA
    x, y, moved, parts, total = pl.pallas_call(
        functools.partial(step_kernel, n),
        out_shape=(
            jax.ShapeDtypeStruct((2, rows, width), BF),
            jax.ShapeDtypeStruct((2, rows, width), BF),
            jax.ShapeDtypeStruct((3, 2 * rows, units), BF),
            jax.ShapeDtypeStruct((n - 1, rows, cols), BF),
            jax.ShapeDtypeStruct((rows, cols), F32),
        ),
        in_specs=[hbm] * 5,
        out_specs=(vmem,) * 5,
        scratch_shapes=[
            pltpu.VMEM((n - 2, rows, width), BF),
            pltpu.VMEM((1, rows, width), BF),
            pltpu.VMEM((units, width), BF),
            pltpu.VMEM((units, width), BF),
            pltpu.VMEM((units, width), BF),
            pltpu.VMEM((n, rows, units), BF),
            pltpu.VMEM((2, 3, rows, units), BF),
            pltpu.VMEM((n, rows, cols), F32),
            pltpu.VMEM((n, rows, cols), F32),
            pltpu.VMEM((n, 2, rows, cols), BF),
            pltpu.VMEM((n, 2, rows, cols), BF),
            pltpu.VMEM((n, rows, cols), BF),
            pltpu.VMEM((n, rows, cols), BF),
            dma((5,)),
            dma((n + 1,)),
            dma((n + 3, 3)),
            dma((n + 3, 4)),
            dma((2,)),
            dma((2,)),
            dma((2, n)),
            dma((2, n)),
        ],
        compiler_params=pltpu.CompilerParams(
            collective_id=0, has_side_effects=True, vmem_limit_bytes=56 * 1024 * 1024
        ),
    )(tokens, out_grad, w_gate, w_up, w_down)

    for at, by in enumerate([-1] + list(range(1, n - 1))):
        total = total + shifted(parts[at], "blk", by).astype(F32)
    x_2 = x.reshape(2 * rows, width)
    y_2 = y.reshape(2 * rows, width)
    return (total.astype(BF), tn(moved[0], x_2), tn(moved[1], x_2), tn(moved[2], y_2))


def solution(mesh):
    square = mesh.shape["inner"] == 4 and mesh.shape["blk"] == 4
    return jax.shard_map(
        on_square if square else on_device,
        mesh=mesh,
        in_specs=(
            P(("groups", "blk"), "inner"),
            P(("groups", "blk"), "inner"),
            P(("blk", "inner"), None),
            P(("blk", "inner"), None),
            P(("blk", "inner"), None),
        ),
        out_specs=(
            P(("groups", "blk"), "inner"),
            P(("groups", "blk", "inner"), None),
            P(("groups", "blk", "inner"), None),
            P(("groups", "blk", "inner"), None),
        ),
        check_vma=False,
    )
```
